1024 devices in a mesh: diamond: 2 (over x_lo), tile: 512 (over y, z, x_hi, core).
Axes of the slice: x: 4 (x_hi: 2, x_lo: 2; x = x_hi * 2 + x_lo), y: 4, z: 32, core: 2. Of those that a mesh axis runs over, the one named last changes fastest.
Arguments:
- adjoint_temp: float32 [2, 512, 256, 128], P('diamond', 'tile'), may hold values from -6 to 6
- misfit: float32 [2, 512, 256, 128], P('diamond', 'tile'), may hold values from -4 to 4
- viscosity: float32 [2, 512, 256, 128], P('diamond', 'tile'), may hold values from 0.1 to 10
- velocity: float32 [3, 2, 512, 256, 128], P(None, 'diamond', 'tile'), may hold values from -6 to 6
- forcing: float32 [3, 2, 512, 256, 128], P(None, 'diamond', 'tile'), may hold values from -9 to 9
- edge_table: int32 [2, 256], replicated, may hold values from 0 to 255, as said below
- pole_table: int32 [2, 256], replicated, may hold values from 0 to 255, as said below
Outputs:
- solution: float32 [3, 2, 512, 256, 128], P(None, 'diamond', 'tile')
- residual: float32 [3, 2, 512, 256, 128], P(None, 'diamond', 'tile')
- adjoint_next: float32 [2, 512, 256, 128], P('diamond', 'tile')
The draws below stay inside these ranges and needn't reach their ends.
Inputs may be any that keep to these rules, and one draw needn't show every extreme that they name: `edge_table`: each row of the table is a permutation of the 256 nodes, and row 1 is the inverse permutation of row 0. `pole_table`: each row of the table is a permutation of the 256 nodes, and row 1 is the inverse permutation of row 0.
All inputs are finite; a program needn't handle non-finite values.
Results may differ from the reference program's by a relative error of at most 0.008.
Values sent between devices are 32-bit elements; how exact they have to be, the bound alone decides.
A program may use at most 32 MiB of HBM per device.

```python
import math
import jax
import jax.numpy as jnp

NY = 256
NR = 128
ITERS = 3
GROUPS = 2
NX = 512


def table_pair(key, count):
    order = jax.random.permutation(key, jnp.arange(count, dtype=jnp.int32))
    inverse = jnp.argsort(order)
    return jnp.stack([order, inverse]).astype(jnp.int32)


def draw_edge_table(key, part):
    key = jax.random.fold_in(key, 11)
    return table_pair(key, NY)


def draw_pole_table(key, part):
    key = jax.random.fold_in(key, 23)
    return table_pair(key, NY)


def draw_forcing(key, part):
    key = jax.random.fold_in(key, 37)
    place = jnp.arange(NX, dtype=jnp.float32) / (NX - 1)
    ramp = place[None, None, :, None, None]
    rough = jnp.clip(jax.random.normal(key, (3, GROUPS, NX, NY, NR), jnp.float32), -5.5, 5.5)
    return rough + 3.0 * ramp


def block_levels(own_key, extent, split, least, largest):
    level, own = 1.0, jax.random.fold_in(own_key, 6)
    for axis_at, shards_of in split:
        draws = jnp.exp(jax.random.uniform(jax.random.fold_in(own, axis_at), (shards_of,), jnp.float32, least / len(split), largest / len(split)))
        level = level * jnp.repeat(draws, extent[axis_at] // shards_of).reshape([-1 if axis == axis_at else 1 for axis in range(len(extent))])
    return level


def gaussian(key, shape, deviation, most, shards=(), kind=jnp.bfloat16):
    array = jax.random.normal(key, shape, jnp.float32) * deviation
    if len(shards) > 0:
        array = block_levels(key, shape, shards, -0.22, 0.18) * array
    return jnp.clip(array, min=-most, max=most).astype(kind)


def setup_inputs(seed: int = 0) -> dict:
    key_list = jax.random.split(jax.random.key(seed), 8)
    adjoint_temp = gaussian(key_list[0], (GROUPS, NX, NY, NR), 1.0, 6.0, ((0, 2), (1, 512)), jnp.float32)
    misfit = gaussian(key_list[1], (GROUPS, NX, NY, NR), 0.5, 4.0, ((0, 2), (1, 512)), jnp.float32)
    viscosity = jnp.clip(jnp.exp(math.log(10.0) - 4.6051702 * jax.random.uniform(key_list[2], (GROUPS, NX, NY, NR), jnp.float32) ** block_levels(key_list[2], (GROUPS, NX, NY, NR), ((0, 2), (1, 512)), -0.2, 0.2)), 0.1, 10.0)
    velocity = gaussian(key_list[3], (3, GROUPS, NX, NY, NR), 1.0, 6.0, ((1, 2), (2, 512)), jnp.float32)
    forcing = draw_forcing(jax.random.fold_in(key_list[7], 71), 0)
    edge_table = draw_edge_table(jax.random.fold_in(key_list[7], 71), 0)
    pole_table = draw_pole_table(jax.random.fold_in(key_list[7], 71), 0)
    return dict(adjoint_temp=adjoint_temp, misfit=misfit, viscosity=viscosity, velocity=velocity, forcing=forcing, edge_table=edge_table, pole_table=pole_table)


TIME_STEP = 0.1
DIFFUSION = 1.0
MASS_TERM = 0.5
BUOYANCY = 1.0


def partner_rows(edge_rows, table):
    flipped = edge_rows[::-1]
    first = jnp.take(flipped[0], table[0], axis=0)
    second = jnp.take(flipped[1], table[1], axis=0)
    return jnp.stack([first, second])


def neighbours(field, edge_table, pole_table):
    x_after = jnp.concatenate([field[:, 1:], partner_rows(field[:, -1], edge_table)[:, None]], axis=1)
    x_before = jnp.concatenate([partner_rows(field[:, 0], pole_table)[:, None], field[:, :-1]], axis=1)
    zeros_y = jnp.zeros_like(field[:, :, :1])
    y_after = jnp.concatenate([field[:, :, 1:], zeros_y], axis=2)
    y_before = jnp.concatenate([zeros_y, field[:, :, :-1]], axis=2)
    zeros_r = jnp.zeros_like(field[:, :, :, :1])
    r_after = jnp.concatenate([field[:, :, :, 1:], zeros_r], axis=3)
    r_before = jnp.concatenate([zeros_r, field[:, :, :, :-1]], axis=3)
    return [x_after, x_before, y_after, y_before, r_after, r_before]


def face_masks(count_y, count_r):
    y_place = jnp.arange(count_y)[:, None]
    r_place = jnp.arange(count_r)
    unity = jnp.ones((1, 1), jnp.float32)
    return [unity, unity,
            (y_place < count_y - 1).astype(jnp.float32), (y_place > 0).astype(jnp.float32),
            (r_place < count_r - 1).astype(jnp.float32), (r_place > 0).astype(jnp.float32)]


def reference(adjoint_temp, misfit, viscosity, velocity, forcing, edge_table, pole_table):
    temp_near = neighbours(adjoint_temp, edge_table, pole_table)
    visc_near = neighbours(viscosity, edge_table, pole_table)
    laplace = sum(temp_near) - 6.0 * adjoint_temp
    transport = 0.5 * (velocity[0] * (temp_near[0] - temp_near[1])
                       + velocity[1] * (temp_near[2] - temp_near[3])
                       + velocity[2] * (temp_near[4] - temp_near[5]))
    adjoint_next = adjoint_temp + TIME_STEP * (DIFFUSION * laplace + transport) + misfit
    inside = face_masks(NY, NR)
    weights = [0.5 * (viscosity + visc_near[k]) * inside[k] for k in range(6)]
    diagonal = MASS_TERM + sum(weights)

    def apply(vector):
        result = []
        for comp in range(3):
            near = neighbours(vector[comp], edge_table, pole_table)
            total = diagonal * vector[comp]
            for k in range(6):
                total = total - weights[k] * near[k]
            result.append(total)
        return jnp.stack(result)

    right = forcing.at[2].add(BUOYANCY * adjoint_next)
    solution = jnp.zeros_like(right)
    residual = right
    precond = residual / diagonal
    direction = precond
    product_now = jnp.sum(residual * precond)
    for step in range(ITERS):
        image = apply(direction)
        step_size = product_now / jnp.sum(direction * image)
        solution = solution + step_size * direction
        residual = residual - step_size * image
        precond = residual / diagonal
        product_next = jnp.sum(residual * precond)
        direction = precond + (product_next / product_now) * direction
        product_now = product_next
    return solution, residual, adjoint_next
```

```python
import functools

import jax
import jax.numpy as jnp
from jax import lax
from jax.experimental import pallas as pl
from jax.experimental.pallas import tpu as pltpu
from jax.sharding import PartitionSpec as P

ITERS = 3
TIME_STEP = 0.1
DIFFUSION = 1.0
MASS_TERM = 0.5
BUOYANCY = 1.0

NY = 256
NR = 128
COMPS = 3
MOMENTS = 2 * ITERS
MESH = pl.DeviceIdType.MESH
NX_CHIPS = 4
NY_CHIPS = 4
NZ_CHIPS = 32
Z_ROUNDS = 4


def device_at(x, y, z, core):
    return (lax.rem(x, 2), ((y * NZ_CHIPS + z) * 2 + x // 2) * 2 + core)


def shift(value, step, axis):
    return pltpu.roll(value, (-step) % value.shape[axis], axis)


def total_of(value):
    return jnp.sum(jnp.sum(value, axis=0, keepdims=True), axis=1, keepdims=True)


def lane_row(entries):
    lane = lax.broadcasted_iota(jnp.int32, (1, NR), 1)
    row = jnp.zeros((1, NR), jnp.float32)
    for k, entry in enumerate(entries):
        row = row + jnp.where(lane == k, entry, 0.0)
    return row


def gradient_coefficients(mu):
    def inner(left, right):
        result = None
        for i, a in enumerate(left):
            for j, b in enumerate(right):
                term = a * b * mu[i + j]
                result = term if result is None else result + term
        return result

    one, zero = jnp.ones_like(mu[0]), jnp.zeros_like(mu[0])
    place, rest, direction = [zero] * ITERS, [one] + [zero] * ITERS, [one]
    now = mu[0]
    for step in range(ITERS):
        image = [direction[0]]
        for i in range(1, len(direction)):
            image.append(direction[i] - direction[i - 1])
        image.append(-direction[-1])
        size = now / inner(direction, image)
        for i, entry in enumerate(direction):
            place[i] = place[i] + size * entry
        for i, entry in enumerate(image):
            rest[i] = rest[i] - size * entry
        if step + 1 < ITERS:
            part = rest[: step + 2]
            later = inner(part, part)
            ratio = later / now
            direction = [part[i] + (ratio * direction[i] if i < len(direction) else 0.0) for i in range(len(part))]
            now = later
    return place, rest


def kernel(
    last,
    temp_in, misfit_in, visc_in, vel_in, forc_in, edge_in, pole_in,
    sol_out, res_out, adj_out,
    temp, misfit, visc, vel, forc, tables, halo0, halo, vs, weights, diag, adj, sol, onehot,
    xbuf, ybuf, zbuf, cbuf, mine,
    load_sem, store_sem, send0, recv0, send, recv, small_send, small_recv, know,
):
    group = lax.axis_index("diamond")
    tile = lax.axis_index("tile")
    core = lax.rem(tile, 2)
    x = lax.rem(tile // 2, 2) * 2 + group
    z = lax.rem(tile // 4, NZ_CHIPS)
    y = tile // (4 * NZ_CHIPS)
    first, final = tile == 0, tile == last

    before_dev = (jnp.where(first, 1 - group, group), jnp.where(first, 0, tile - 1))
    after_dev = (jnp.where(final, 1 - group, group), jnp.where(final, last, tile + 1))
    side_dev = (before_dev, after_dev)
    side_slot = (jnp.where(first, 0, 1), jnp.where(final, 1, 0))

    def x_dev(i):
        return device_at(x ^ i, y, z, core)

    def y_dev(i):
        return device_at(x, y ^ i, z, core)

    def z_dev(i):
        return device_at(x, y, lax.rem(z + i + NZ_CHIPS, NZ_CHIPS), core)

    loads = [
        pltpu.make_async_copy(source, target, load_sem.at[i])
        for i, (source, target) in enumerate(
            ((visc_in, visc), (temp_in, temp), (forc_in, forc), (misfit_in, misfit), (vel_in, vel), (edge_in, tables.at[1]), (pole_in, tables.at[0]))
        )
    ]
    for load in loads:
        load.start()

    barrier = pltpu.get_barrier_semaphore()
    greeted = [*side_dev, x_dev(1), x_dev(3), y_dev(1), y_dev(3), z_dev(-1), z_dev(1)]
    for dev in greeted:
        pl.semaphore_signal(barrier, inc=1, device_id=dev, device_id_type=MESH)
    pl.semaphore_wait(barrier, len(greeted))

    def first_copy(side, k):
        return pltpu.make_async_remote_copy(
            src_ref=(visc_in, temp_in)[k],
            dst_ref=halo0.at[side_slot[side], k],
            send_sem=send0.at[side, k],
            recv_sem=recv0.at[side_slot[side], k],
            device_id=side_dev[side],
            device_id_type=MESH,
        )

    def first_arrival(side, k):
        pltpu.make_async_remote_copy(
            src_ref=halo0.at[side, k],
            dst_ref=halo0.at[side, k],
            send_sem=send0.at[side, k],
            recv_sem=recv0.at[side, k],
            device_id=side_dev[side],
            device_id_type=MESH,
        ).wait_recv()

    def row_copy(step, side, c):
        return pltpu.make_async_remote_copy(
            src_ref=vs.at[step, c],
            dst_ref=halo.at[step, side_slot[side], c],
            send_sem=send.at[step, side, c],
            recv_sem=recv.at[step, side_slot[side], c],
            device_id=side_dev[side],
            device_id_type=MESH,
        )

    def row_arrival(step, side, c):
        pltpu.make_async_remote_copy(
            src_ref=halo.at[step, side, c],
            dst_ref=halo.at[step, side, c],
            send_sem=send.at[step, side, c],
            recv_sem=recv.at[step, side, c],
            device_id=side_dev[side],
            device_id_type=MESH,
        ).wait_recv()

    def reorder(ref, side):
        @pl.when((first, final)[side])
        def _():
            ref[...] = jnp.dot(onehot[...], ref[...], precision=lax.Precision.HIGHEST, preferred_element_type=jnp.float32)

    for k in range(2):
        for side in range(2):
            first_copy(side, k).start()

    def tell(round_, devs):
        for dev in devs:
            pl.semaphore_signal(know.at[round_], inc=1, device_id=dev, device_id_type=MESH)

    def hear(round_):
        pl.semaphore_wait(know.at[round_], 2)

    tell(0, (z_dev(-1), z_dev(1)))
    tell(Z_ROUNDS, (x_dev(1), x_dev(3)))
    tell(Z_ROUNDS + 1, (y_dev(1), y_dev(3)))

    loads[5].wait()
    loads[6].wait()

    for side in range(2):

        @pl.when((first, final)[side])
        def _():
            inverse = jnp.where(group == 0, tables[side, 1:2, :], tables[side, 0:1, :])
            place = lax.broadcasted_iota(jnp.int32, (NY, NY), 0)
            onehot[...] = jnp.where(place == inverse, 1.0, 0.0).astype(jnp.float32)

    y_place = lax.broadcasted_iota(jnp.int32, (NY, NR), 0)
    r_place = lax.broadcasted_iota(jnp.int32, (NY, NR), 1)
    inside = (y_place < NY - 1, y_place > 0, r_place < NR - 1, r_place > 0)
    moves = ((1, 0), (-1, 0), (1, 1), (-1, 1))

    loads[0].wait()
    own = visc[...]
    rowwise = MASS_TERM
    for k, (step, axis) in enumerate(moves):
        weight = jnp.where(inside[k], 0.5 * (own + shift(own, step, axis)), 0.0)
        weights[2 + k] = weight
        rowwise = rowwise + weight
    diag[...] = rowwise

    for side in range(2):
        first_arrival(side, 0)
        reorder(halo0.at[side, 0], side)
    after = 0.5 * (visc[...] + halo0[1, 0])
    before = 0.5 * (visc[...] + halo0[0, 0])
    diagonal = diag[...] + after + before
    diag[...] = diagonal
    inverse_diagonal = 1.0 / diagonal
    weights[0] = after * inverse_diagonal
    weights[1] = before * inverse_diagonal
    for k in range(2, 6):
        weights[k] = weights[k] * inverse_diagonal

    loads[2].wait()
    for c in range(COMPS - 1):
        vs[0, c] = forc[c] / diag[...]
        for side in range(2):
            row_copy(0, side, c).start()

    loads[1].wait()
    loads[3].wait()
    loads[4].wait()
    own = temp[...]
    near = [jnp.where(inside[k], shift(own, step, axis), 0.0) for k, (step, axis) in enumerate(moves)]
    rowwise = own + misfit[...] + TIME_STEP * (
        DIFFUSION * (near[0] + near[1] + near[2] + near[3] - 6.0 * own)
        + 0.5 * (vel[1] * (near[0] - near[1]) + vel[2] * (near[2] - near[3]))
    )
    adj[...] = rowwise
    for side in range(2):
        first_arrival(side, 1)
        reorder(halo0.at[side, 1], side)
    after, before = halo0[1, 1], halo0[0, 1]
    adj[...] = adj[...] + TIME_STEP * (DIFFUSION * (after + before) + 0.5 * (vel[0] * (after - before)))
    vs[0, COMPS - 1] = (forc[COMPS - 1] + BUOYANCY * adj[...]) / diag[...]
    for side in range(2):
        row_copy(0, side, COMPS - 1).start()
    adj_store = pltpu.make_async_copy(adj, adj_out, store_sem.at[2])
    adj_store.start()

    hear(0)
    tell(1, (z_dev(-2), z_dev(2)))

    def in_row(step, c):
        value = vs[step, c]
        result = None
        for k, (move, axis) in enumerate(moves):
            term = weights[2 + k] * shift(value, move, axis)
            result = term if result is None else result + term
        vs[step + 1, c] = result

    mu = []
    for step in range(ITERS - 1):
        for c in range(COMPS):
            in_row(step, c)
        even = diag[...] * sum(vs[step, c] * vs[step, c] for c in range(COMPS))
        mu.append(total_of(even))
        for c in range(COMPS):
            for side in range(2):
                row_arrival(step, side, c)
                reorder(halo.at[step, side, c], side)
            vs[step + 1, c] = vs[step + 1, c] + weights[0] * halo[step, 1, c] + weights[1] * halo[step, 0, c]
            row_copy(step + 1, 1, c).start()
            if step + 2 < ITERS:
                row_copy(step + 1, 0, c).start()
            else:

                @pl.when(first)
                def _():
                    row_copy(step + 1, 0, c).start()

        odd = diag[...] * sum(vs[step, c] * vs[step + 1, c] for c in range(COMPS))
        mu.append(total_of(odd))
        hear(1 + step)
        tell(2 + step, (z_dev(-(4 << step)), z_dev(4 << step)))
        if step == 0:
            hear(Z_ROUNDS)
            hear(Z_ROUNDS + 1)

    step = ITERS - 1
    for c in range(COMPS):
        in_row(step, c)
    mu.append(total_of(diag[...] * sum(vs[step, c] * vs[step, c] for c in range(COMPS))))
    inner_part = sum(vs[step, c] * vs[step + 1, c] for c in range(COMPS))
    edges = None
    for c in range(COMPS):
        row_arrival(step, 0, c)
        reorder(halo.at[step, 0, c], 0)
        part = weights[1] * halo[step, 0, c]
        vs[step + 1, c] = vs[step + 1, c] + part
        term = vs[step, c] * part
        edges = term if edges is None else edges + term
    count = jnp.where(first, 1.0, 2.0)
    mu.append(total_of(diag[...] * (inner_part + count * edges)))
    mine[...] = lane_row(mu)

    @pl.when(final)
    def _():
        edges = None
        for c in range(COMPS):
            row_arrival(step, 1, c)
            reorder(halo.at[step, 1, c], 1)
            term = vs[step, c] * halo[step, 1, c]
            edges = term if edges is None else edges + term
        mine[...] = mine[...] + lane_row([0.0] * (MOMENTS - 1) + [total_of(diag[...] * weights[0] * edges)])

    def small_copy(i, buffer, slot, dev):
        return pltpu.make_async_remote_copy(
            src_ref=mine, dst_ref=buffer.at[slot], send_sem=small_send.at[i], recv_sem=small_recv.at[i], device_id=dev, device_id_type=MESH
        )

    def spread(i, buffer, slot, devs):
        buffer[slot] = mine[...]
        for dev in devs:
            small_copy(i, buffer, slot, dev).start()

    def gather(i, buffer, count):
        shape = buffer.at[pl.ds(0, count)]
        whole = pltpu.make_async_remote_copy(
            src_ref=shape, dst_ref=shape, send_sem=small_send.at[i], recv_sem=small_recv.at[i], device_id=x_dev(1), device_id_type=MESH
        )
        whole.wait_send()
        whole.wait_recv()
        mine[...] = jnp.sum(buffer[...], axis=0)

    spread(0, cbuf, core, [device_at(x, y, z, 1 - core)])
    gather(0, cbuf, 1)
    spread(1, xbuf, x, [x_dev(2), x_dev(1), x_dev(3)])
    gather(1, xbuf, NX_CHIPS - 1)
    spread(2, ybuf, y, [y_dev(2), y_dev(1), y_dev(3)])
    gather(2, ybuf, NY_CHIPS - 1)
    hear(Z_ROUNDS - 1)
    zbuf[z] = mine[...]

    def z_send(i, carry):
        k = (i + 1) // 2
        offset = NZ_CHIPS // 2 + k * (1 - 2 * lax.rem(i, 2))
        small_copy(3, zbuf, z, z_dev(offset)).start()
        return carry

    lax.fori_loop(0, NZ_CHIPS - 1, z_send, 0)

    for c in range(COMPS):

        @pl.when(jnp.logical_not(first))
        def _():
            row_copy(step, 0, c).start()

    for c in range(COMPS):

        @pl.when(jnp.logical_not(final))
        def _():
            row_arrival(step, 1, c)

        vs[step + 1, c] = vs[step + 1, c] + weights[0] * halo[step, 1, c]

    gather(3, zbuf, NZ_CHIPS - 1)
    sums = mine[...]
    place, rest = gradient_coefficients([sums[:, k : k + 1] for k in range(MOMENTS)])
    for c in range(COMPS):
        sol[0, c] = sum(place[k] * vs[k, c] for k in range(ITERS))
    sol_store = pltpu.make_async_copy(sol.at[0], sol_out, store_sem.at[0])
    sol_store.start()
    for c in range(COMPS):
        sol[1, c] = diag[...] * sum(rest[k] * vs[k, c] for k in range(ITERS + 1))
    res_store = pltpu.make_async_copy(sol.at[1], res_out, store_sem.at[1])
    res_store.start()

    for k in range(2):
        for side in range(2):
            first_copy(side, k).wait_send()
    for s in range(ITERS):
        for side in range(2):
            for c in range(COMPS):
                row_copy(s, side, c).wait_send()
    adj_store.wait()
    sol_store.wait()
    res_store.wait()


def body(adjoint_temp, misfit, viscosity, velocity, forcing, edge_table, pole_table):
    row = (NY, NR)
    rows = (COMPS, NY, NR)
    f32 = jnp.float32
    any_space = pl.BlockSpec(memory_space=pl.ANY)
    sol, res, adj = pl.pallas_call(
        functools.partial(kernel, lax.axis_size("tile") - 1),
        out_shape=(
            jax.ShapeDtypeStruct(rows, f32),
            jax.ShapeDtypeStruct(rows, f32),
            jax.ShapeDtypeStruct(row, f32),
        ),
        in_specs=[any_space] * 7,
        out_specs=(any_space,) * 3,
        scratch_shapes=[
            pltpu.VMEM(row, f32),
            pltpu.VMEM(row, f32),
            pltpu.VMEM(row, f32),
            pltpu.VMEM(rows, f32),
            pltpu.VMEM(rows, f32),
            pltpu.VMEM((2, 2, NY), jnp.int32),
            pltpu.VMEM((2, 2, *row), f32),
            pltpu.VMEM((ITERS, 2, *rows), f32),
            pltpu.VMEM((ITERS + 1, *rows), f32),
            pltpu.VMEM((6, *row), f32),
            pltpu.VMEM(row, f32),
            pltpu.VMEM(row, f32),
            pltpu.VMEM((2, *rows), f32),
            pltpu.VMEM((NY, NY), f32),
            pltpu.VMEM((NX_CHIPS, 1, NR), f32),
            pltpu.VMEM((NY_CHIPS, 1, NR), f32),
            pltpu.VMEM((NZ_CHIPS, 1, NR), f32),
            pltpu.VMEM((2, 1, NR), f32),
            pltpu.VMEM((1, NR), f32),
            pltpu.SemaphoreType.DMA((7,)),
            pltpu.SemaphoreType.DMA((3,)),
            pltpu.SemaphoreType.DMA((2, 2)),
            pltpu.SemaphoreType.DMA((2, 2)),
            pltpu.SemaphoreType.DMA((ITERS, 2, COMPS)),
            pltpu.SemaphoreType.DMA((ITERS, 2, COMPS)),
            pltpu.SemaphoreType.DMA((4,)),
            pltpu.SemaphoreType.DMA((4,)),
            pltpu.SemaphoreType.REGULAR((Z_ROUNDS + 2,)),
        ],
        compiler_params=pltpu.CompilerParams(collective_id=0, has_side_effects=True, vmem_limit_bytes=32 << 20),
    )(
        adjoint_temp.reshape(row),
        misfit.reshape(row),
        viscosity.reshape(row),
        velocity.reshape(rows),
        forcing.reshape(rows),
        edge_table,
        pole_table,
    )
    shape = adjoint_temp.shape
    return sol.reshape((COMPS, *shape)), res.reshape((COMPS, *shape)), adj.reshape(shape)


def solution(mesh):
    placed = (
        P("diamond", "tile", None, None),
        P("diamond", "tile", None, None),
        P("diamond", "tile", None, None),
        P(None, "diamond", "tile", None, None),
        P(None, "diamond", "tile", None, None),
        P(),
        P(),
    )
    return jax.shard_map(
        body,
        mesh=mesh,
        in_specs=placed,
        out_specs=(
            P(None, "diamond", "tile", None, None),
            P(None, "diamond", "tile", None, None),
            P("diamond", "tile", None, None),
        ),
        check_vma=False,
    )
```

```python
import functools

import jax
import jax.numpy as jnp
from jax import lax
from jax.experimental import pallas as pl
from jax.experimental.pallas import tpu as pltpu
from jax.sharding import PartitionSpec as P

ITERS = 3
TIME_STEP = 0.1
DIFFUSION = 1.0
MASS_TERM = 0.5
BUOYANCY = 1.0

NY = 256
NR = 128
HALF = NY // 2
COMPS = 3
MOMENTS = 2 * ITERS
MESH = pl.DeviceIdType.MESH
NX_CHIPS = 4
NY_CHIPS = 4
NZ_CHIPS = 32
Z_ROUNDS = 4


def device_at(x, y, z, core):
    return (lax.rem(x, 2), ((y * NZ_CHIPS + z) * 2 + x // 2) * 2 + core)


def shift(value, step, axis):
    return pltpu.roll(value, (-step) % value.shape[axis], axis)


def total_of(value):
    return jnp.sum(jnp.sum(value[0] + value[1], axis=0, keepdims=True), axis=1, keepdims=True)


def lane_row(entries):
    lane = lax.broadcasted_iota(jnp.int32, (1, NR), 1)
    row = jnp.zeros((1, NR), jnp.float32)
    for k, entry in enumerate(entries):
        row = row + jnp.where(lane == k, entry, 0.0)
    return row


def gradient_coefficients(mu):
    def inner(left, right):
        result = None
        for i, a in enumerate(left):
            for j, b in enumerate(right):
                term = a * b * mu[i + j]
                result = term if result is None else result + term
        return result

    one, zero = jnp.ones_like(mu[0]), jnp.zeros_like(mu[0])
    place, rest, direction = [zero] * ITERS, [one] + [zero] * ITERS, [one]
    now = mu[0]
    for step in range(ITERS):
        image = [direction[0]]
        for i in range(1, len(direction)):
            image.append(direction[i] - direction[i - 1])
        image.append(-direction[-1])
        size = now / inner(direction, image)
        for i, entry in enumerate(direction):
            place[i] = place[i] + size * entry
        for i, entry in enumerate(image):
            rest[i] = rest[i] - size * entry
        if step + 1 < ITERS:
            part = rest[: step + 2]
            later = inner(part, part)
            ratio = later / now
            direction = [part[i] + (ratio * direction[i] if i < len(direction) else 0.0) for i in range(len(part))]
            now = later
    return place, rest


def kernel(
    last,
    temp_in, misfit_in, visc_in, vel_in, forc_in, edge_in, pole_in,
    sol_out, res_out, adj_out,
    temp, misfit, vel, forc, tables, beside, moved, near, partner, line_out, line_in, vs, weights, far, diag, adj, right, home, sol, onehot,
    xbuf, ybuf, zbuf, cbuf, mine,
    load_sem, store_sem, temp_send, temp_recv, move_send, move_recv, move_own, in_send, in_recv, out_send, out_recv, line_send, line_recv,
    back_send, back_recv, small_send, small_recv, know,
):
    group = lax.axis_index("diamond")
    tile = lax.axis_index("tile")
    core = lax.rem(tile, 2)
    half = lax.rem(tile // 2, 2)
    quad = tile // 4
    x = half * 2 + group
    z = lax.rem(quad, NZ_CHIPS)
    y = quad // NZ_CHIPS
    first, final = tile == 0, tile == last
    opens = jnp.logical_and(quad == 0, core == 0)
    closes = jnp.logical_and(quad == last // 4, core == 1)
    at_end = jnp.logical_or(opens, closes)
    within = jnp.logical_not(at_end)
    outer_home = core == half

    def quad_dev(which_half, which_core):
        return (group, quad * 4 + which_half * 2 + which_core)

    def partner_dev(which_half):
        return (1 - group, quad * 4 + which_half * 2 + core)

    def x_dev(i):
        return device_at(x ^ i, y, z, core)

    def y_dev(i):
        return device_at(x, y ^ i, z, core)

    def z_dev(i):
        return device_at(x, y, lax.rem(z + i + NZ_CHIPS, NZ_CHIPS), core)

    inner_dev = quad_dev(half, 1 - core)
    outer_dev = (group, jnp.where(at_end, tile, jnp.where(core == 0, tile - 3, tile + 3)))
    line_dev = quad_dev(1 - half, core)
    before_dev = (jnp.where(first, 1 - group, group), jnp.where(first, 0, tile - 1))
    after_dev = (jnp.where(final, 1 - group, group), jnp.where(final, last, tile + 1))
    side_dev = (before_dev, after_dev)
    side_slot = (jnp.where(first, 0, 1), jnp.where(final, 1, 0))
    here = pl.ds(pl.multiple_of(half * HALF, HALF), HALF)

    loads = [
        pltpu.make_async_copy(source, target, load_sem.at[i])
        for i, (source, target) in enumerate(
            ((temp_in, temp), (misfit_in, misfit), (vel_in, vel), (forc_in, forc), (edge_in, tables.at[1]), (pole_in, tables.at[0]))
        )
    ]
    for load in loads:
        load.start()

    barrier = pltpu.get_barrier_semaphore()

    def greet(dev):
        pl.semaphore_signal(barrier, inc=1, device_id=dev, device_id_type=MESH)

    greeted = [inner_dev, line_dev, quad_dev(1 - half, 1 - core), x_dev(1), x_dev(3), y_dev(1), y_dev(3), z_dev(-1), z_dev(1)]
    for dev in greeted:
        greet(dev)
    home_beside = jnp.logical_and(outer_home, within)

    @pl.when(within)
    def _():
        greet(outer_dev)

    @pl.when(home_beside)
    def _():
        greet((group, jnp.where(core == 0, tile - 1, tile + 1)))

    @pl.when(at_end)
    def _():
        greet(partner_dev(0))
        greet(partner_dev(1))

    pl.semaphore_wait(barrier, len(greeted) + jnp.where(at_end, 2, jnp.where(home_beside, 2, 1)))

    def remote(source, target, send_sem, recv_sem, dev):
        return pltpu.make_async_remote_copy(
            src_ref=source, dst_ref=target, send_sem=send_sem, recv_sem=recv_sem, device_id=dev, device_id_type=MESH
        )

    def arrived(target, recv_sem):
        remote(target, target, temp_send.at[0], recv_sem, inner_dev).wait_recv()

    def temp_copy(side):
        return remote(temp_in, beside.at[side_slot[side]], temp_send.at[side], temp_recv.at[side_slot[side]], side_dev[side])

    sources = [visc_in, forc_in.at[0], forc_in.at[1], right]
    slot = jnp.where(outer_home, 0, 1)

    def move_copy(f, h):
        return remote(sources[f].at[pl.ds(h * HALF, HALF)], moved.at[f, slot], move_send.at[f, h], move_recv.at[f, slot], quad_dev(h, half))

    def own_copy(f):
        return pltpu.make_async_copy(sources[f].at[here], moved.at[f, 0], move_own.at[f])

    def move(f):
        for h in range(2):

            @pl.when(jnp.logical_not(jnp.logical_and(outer_home, half == h)))
            def _():
                move_copy(f, h).start()

        @pl.when(outer_home)
        def _():
            own_copy(f).start()

    def move_sent(f):
        for h in range(2):

            @pl.when(jnp.logical_not(jnp.logical_and(outer_home, half == h)))
            def _():
                move_copy(f, h).wait_send()

    def move_done(f):
        @pl.when(outer_home)
        def _():
            own_copy(f).wait()

        @pl.when(jnp.logical_not(outer_home))
        def _():
            arrived(moved.at[f, 0], move_recv.at[f, 0])

        arrived(moved.at[f, 1], move_recv.at[f, 1])

    def in_copy(s, c, rows):
        return remote(rows.at[1], near.at[s, c, 1], in_send.at[s, c], in_recv.at[s, c], inner_dev)

    def out_copy(s, c, rows):
        return remote(rows.at[0], near.at[s, c, 0], out_send.at[s, c, 0], out_recv.at[s, c, 0], outer_dev)

    def end_copy(s, c, rows, h):
        return remote(rows.at[0], partner.at[s, c, here], out_send.at[s, c, h], out_recv.at[s, c, half], partner_dev(h))

    def line_copy(s, c):
        return remote(line_out.at[s, c], line_in.at[s, c], line_send.at[s, c], line_recv.at[s, c], line_dev)

    def give(s, c, rows):
        @pl.when(within)
        def _():
            out_copy(s, c, rows).start()

        @pl.when(at_end)
        def _():
            for h in range(2):
                end_copy(s, c, rows, h).start()

        line_out[s, c] = jnp.where(half == 0, rows[:, HALF - 1 : HALF, :], rows[:, 0:1, :])
        line_copy(s, c).start()
        in_copy(s, c, rows).start()

    def given(s, c, rows):
        @pl.when(within)
        def _():
            out_copy(s, c, rows).wait_send()

        @pl.when(at_end)
        def _():
            for h in range(2):
                end_copy(s, c, rows, h).wait_send()

        line_copy(s, c).wait_send()
        in_copy(s, c, rows).wait_send()

    def take(s, c):
        arrived(near.at[s, c, 1], in_recv.at[s, c])
        arrived(line_in.at[s, c], line_recv.at[s, c])

        @pl.when(within)
        def _():
            arrived(near.at[s, c, 0], out_recv.at[s, c, 0])

        @pl.when(at_end)
        def _():
            for h in range(2):
                arrived(partner.at[s, c, pl.ds(h * HALF, HALF)], out_recv.at[s, c, h])
            near[s, c, 0] = jnp.dot(
                onehot[here, :], partner[s, c], precision=lax.Precision.HIGHEST, preferred_element_type=jnp.float32
            )

    def back_copy(a, rows, p):
        return remote(
            rows.at[p], home.at[a, here], back_send.at[a, p], back_recv.at[a, half], quad_dev(core, (core, 1 - core)[p])
        )

    def give_back(a, rows):
        @pl.when(outer_home)
        def _():
            home[a, here, :] = rows[0]

        @pl.when(jnp.logical_not(outer_home))
        def _():
            back_copy(a, rows, 0).start()

        back_copy(a, rows, 1).start()

    def back_sent(a, rows):
        @pl.when(jnp.logical_not(outer_home))
        def _():
            back_copy(a, rows, 0).wait_send()

        back_copy(a, rows, 1).wait_send()

    def back_done(a):
        for h in range(2):

            @pl.when(jnp.logical_not(jnp.logical_and(outer_home, half == h)))
            def _():
                arrived(home.at[a, pl.ds(h * HALF, HALF)], back_recv.at[a, h])

    for side in range(2):
        temp_copy(side).start()
    for f in range(3):
        move(f)

    def tell(round_, devs):
        for dev in devs:
            pl.semaphore_signal(know.at[round_], inc=1, device_id=dev, device_id_type=MESH)

    def hear(round_):
        pl.semaphore_wait(know.at[round_], 2)

    tell(0, (z_dev(-1), z_dev(1)))
    tell(Z_ROUNDS, (x_dev(1), x_dev(3)))
    tell(Z_ROUNDS + 1, (y_dev(1), y_dev(3)))

    loads[4].wait()
    loads[5].wait()

    for at, end in enumerate((opens, closes)):

        @pl.when(end)
        def _():
            inverse = jnp.where(group == 0, tables[at, 1:2, :], tables[at, 0:1, :])
            place = lax.broadcasted_iota(jnp.int32, (NY, NY), 0)
            onehot[...] = jnp.where(place == inverse, 1.0, 0.0).astype(jnp.float32)

    for load in loads[:4]:
        load.wait()
    y_place = lax.broadcasted_iota(jnp.int32, (NY, NR), 0)
    r_place = lax.broadcasted_iota(jnp.int32, (NY, NR), 1)
    inside = (y_place < NY - 1, y_place > 0, r_place < NR - 1, r_place > 0)
    own = temp[...]
    other = [jnp.where(inside[k], shift(own, step, axis), 0.0) for k, (step, axis) in enumerate(((1, 0), (-1, 0), (1, 1), (-1, 1)))]
    adj[...] = own + misfit[...] + TIME_STEP * (
        DIFFUSION * (other[0] + other[1] + other[2] + other[3] - 6.0 * own)
        + 0.5 * (vel[1] * (other[0] - other[1]) + vel[2] * (other[2] - other[3]))
    )
    for side in range(2):
        arrived(beside.at[side], temp_recv.at[side])

        @pl.when((first, final)[side])
        def _():
            beside[side] = jnp.dot(onehot[...], beside[side], precision=lax.Precision.HIGHEST, preferred_element_type=jnp.float32)

    after, before = beside[1], beside[0]
    adj[...] = adj[...] + TIME_STEP * (DIFFUSION * (after + before) + 0.5 * (vel[0] * (after - before)))
    right[...] = forc[COMPS - 1] + BUOYANCY * adj[...]
    move(3)
    adj_store = pltpu.make_async_copy(adj, adj_out, store_sem.at[2])
    adj_store.start()
    hear(0)
    tell(1, (z_dev(-2), z_dev(2)))

    moves = ((1, 1), (-1, 1), (1, 2), (-1, 2))
    shape = (2, HALF, NR)
    y_place = lax.broadcasted_iota(jnp.int32, shape, 1)
    r_place = lax.broadcasted_iota(jnp.int32, shape, 2)
    inside = (y_place < HALF - 1, y_place > 0, r_place < NR - 1, r_place > 0)
    move_done(0)
    visc = moved.at[0]
    give(ITERS, 0, visc)
    own = visc[...]
    local = jnp.full(shape, MASS_TERM, jnp.float32)
    for k, (step, axis) in enumerate(moves):
        weight = jnp.where(inside[k], 0.5 * (own + shift(own, step, axis)), 0.0)
        weights[k] = weight
        local = local + weight
    between = 0.5 * (own[0] + own[1])
    for p in range(2):
        weights[4, p] = between
    diag[...] = local + weights[4]
    take(ITERS, 0)
    border = line_in[ITERS, 0]
    for at, (place, own_half) in enumerate(((HALF - 1, 0), (0, 1))):
        rows = slice(place, place + 1)
        weight = jnp.where(half == own_half, 0.5 * (visc[:, rows, :] + border), 0.0)
        diag[:, rows, :] = diag[:, rows, :] + weight
        far[at] = weight
    outside = 0.5 * (visc[...] + near[ITERS, 0])
    diagonal = diag[...] + outside
    diag[...] = diagonal
    inverse_diagonal = 1.0 / diagonal
    weights[5] = outside * inverse_diagonal
    for k in range(5):
        weights[k] = weights[k] * inverse_diagonal
    for at, place in enumerate((HALF - 1, 0)):
        far[at] = far[at] * inverse_diagonal[:, place : place + 1, :]

    for c in range(COMPS):
        move_done(1 + c)
        vs[0, c] = moved[1 + c] / diag[...]
        give(0, c, vs.at[0, c])

    mu = []
    for step in range(ITERS):
        for c in range(COMPS):
            value = vs[step, c]
            result = weights[4, 0] * value[1], weights[4, 1] * value[0]
            vs[step + 1, c, 0] = result[0]
            vs[step + 1, c, 1] = result[1]
            part = vs[step + 1, c]
            for k, (move_by, axis) in enumerate(moves):
                part = part + weights[k] * shift(value, move_by, axis)
            vs[step + 1, c] = part
        mu.append(total_of(diag[...] * sum(vs[step, c] * vs[step, c] for c in range(COMPS))))
        for c in range(COMPS):
            take(step, c)
            vs[step + 1, c] = vs[step + 1, c] + weights[5] * near[step, c]
            for at, place in enumerate((HALF - 1, 0)):
                rows = slice(place, place + 1)
                vs[step + 1, c, :, rows, :] = vs[step + 1, c, :, rows, :] + far[at] * line_in[step, c]
            if step + 1 < ITERS:
                give(step + 1, c, vs.at[step + 1, c])
        mu.append(total_of(diag[...] * sum(vs[step, c] * vs[step + 1, c] for c in range(COMPS))))
        if step + 1 < ITERS:
            if step == 0:
                give_back(0, diag)
                hear(Z_ROUNDS)
                hear(Z_ROUNDS + 1)
            for c in range(COMPS):
                give_back(1 + step * COMPS + c, vs.at[step + 1, c])
            hear(1 + step)
            tell(2 + step, (z_dev(-(4 << step)), z_dev(4 << step)))

    def small_copy(i, buffer, slot, dev):
        return remote(mine, buffer.at[slot], small_send.at[i], small_recv.at[i], dev)

    def spread(i, buffer, slot, devs):
        buffer[slot] = mine[...]
        for dev in devs:
            small_copy(i, buffer, slot, dev).start()

    def gather(i, buffer, count):
        part = buffer.at[pl.ds(0, count)]
        whole = remote(part, part, small_send.at[i], small_recv.at[i], inner_dev)
        whole.wait_send()
        whole.wait_recv()
        mine[...] = jnp.sum(buffer[...], axis=0)

    mine[...] = lane_row(mu)
    hear(Z_ROUNDS - 1)
    zbuf[z] = mine[...]

    def z_send(i, carry):
        k = (i + 1) // 2
        offset = NZ_CHIPS // 2 + k * (1 - 2 * lax.rem(i, 2))
        small_copy(3, zbuf, z, z_dev(offset)).start()
        return carry

    lax.fori_loop(0, NZ_CHIPS - 1, z_send, 0)
    for c in range(COMPS):
        give_back(1 + (ITERS - 1) * COMPS + c, vs.at[ITERS, c])
    gather(3, zbuf, NZ_CHIPS - 1)
    spread(0, cbuf, core, [inner_dev])
    gather(0, cbuf, 1)
    spread(1, xbuf, x, [x_dev(2), x_dev(1), x_dev(3)])
    gather(1, xbuf, NX_CHIPS - 1)
    spread(2, ybuf, y, [y_dev(2), y_dev(1), y_dev(3)])
    for a in range(1 + ITERS * COMPS):
        back_done(a)
    gather(2, ybuf, NY_CHIPS - 1)
    sums = mine[...]
    place, rest = gradient_coefficients([sums[:, k : k + 1] for k in range(MOMENTS)])
    for c in range(COMPS):
        full = forc[c] if c + 1 < COMPS else right[...]
        krylov = [full / home[0]] + [home[1 + step * COMPS + c] for step in range(ITERS)]
        sol[0, c] = sum(place[k] * krylov[k] for k in range(ITERS))
        sol[1, c] = rest[0] * full + home[0] * sum(rest[k] * krylov[k] for k in range(1, ITERS + 1))
    sol_store = pltpu.make_async_copy(sol.at[0], sol_out, store_sem.at[0])
    sol_store.start()
    res_store = pltpu.make_async_copy(sol.at[1], res_out, store_sem.at[1])
    res_store.start()

    for side in range(2):
        temp_copy(side).wait_send()
    for f in range(1 + COMPS):
        move_sent(f)
    given(ITERS, 0, visc)
    back_sent(0, diag)
    for s in range(ITERS):
        for c in range(COMPS):
            given(s, c, vs.at[s, c])
            back_sent(1 + s * COMPS + c, vs.at[s + 1, c])
    adj_store.wait()
    sol_store.wait()
    res_store.wait()


def body(adjoint_temp, misfit, viscosity, velocity, forcing, edge_table, pole_table):
    row = (NY, NR)
    rows = (COMPS, NY, NR)
    pair = (2, HALF, NR)
    f32 = jnp.float32
    dma = pltpu.SemaphoreType.DMA
    any_space = pl.BlockSpec(memory_space=pl.ANY)
    sol, res, adj = pl.pallas_call(
        functools.partial(kernel, lax.axis_size("tile") - 1),
        out_shape=(
            jax.ShapeDtypeStruct(rows, f32),
            jax.ShapeDtypeStruct(rows, f32),
            jax.ShapeDtypeStruct(row, f32),
        ),
        in_specs=[any_space] * 7,
        out_specs=(any_space,) * 3,
        scratch_shapes=[
            pltpu.VMEM(row, f32),
            pltpu.VMEM(row, f32),
            pltpu.VMEM(rows, f32),
            pltpu.VMEM(rows, f32),
            pltpu.VMEM((2, 2, NY), jnp.int32),
            pltpu.VMEM((2, *row), f32),
            pltpu.VMEM((1 + COMPS, *pair), f32),
            pltpu.VMEM((ITERS + 1, COMPS, *pair), f32),
            pltpu.VMEM((ITERS + 1, COMPS, *row), f32),
            pltpu.VMEM((ITERS + 1, COMPS, 2, 1, NR), f32),
            pltpu.VMEM((ITERS + 1, COMPS, 2, 1, NR), f32),
            pltpu.VMEM((ITERS + 1, COMPS, *pair), f32),
            pltpu.VMEM((6, *pair), f32),
            pltpu.VMEM((2, 2, 1, NR), f32),
            pltpu.VMEM(pair, f32),
            pltpu.VMEM(row, f32),
            pltpu.VMEM(row, f32),
            pltpu.VMEM((1 + ITERS * COMPS, *row), f32),
            pltpu.VMEM((2, *rows), f32),
            pltpu.VMEM((NY, NY), f32),
            pltpu.VMEM((NX_CHIPS, 1, NR), f32),
            pltpu.VMEM((NY_CHIPS, 1, NR), f32),
            pltpu.VMEM((NZ_CHIPS, 1, NR), f32),
            pltpu.VMEM((2, 1, NR), f32),
            pltpu.VMEM((1, NR), f32),
            dma((6,)),
            dma((3,)),
            dma((2,)),
            dma((2,)),
            dma((1 + COMPS, 2)),
            dma((1 + COMPS, 2)),
            dma((1 + COMPS,)),
            dma((ITERS + 1, COMPS)),
            dma((ITERS + 1, COMPS)),
            dma((ITERS + 1, COMPS, 2)),
            dma((ITERS + 1, COMPS, 2)),
            dma((ITERS + 1, COMPS)),
            dma((ITERS + 1, COMPS)),
            dma((1 + ITERS * COMPS, 2)),
            dma((1 + ITERS * COMPS, 2)),
            dma((4,)),
            dma((4,)),
            pltpu.SemaphoreType.REGULAR((Z_ROUNDS + 2,)),
        ],
        compiler_params=pltpu.CompilerParams(collective_id=0, has_side_effects=True, vmem_limit_bytes=60 << 20),
    )(
        adjoint_temp.reshape(row),
        misfit.reshape(row),
        viscosity.reshape(row),
        velocity.reshape(rows),
        forcing.reshape(rows),
        edge_table,
        pole_table,
    )
    shape = adjoint_temp.shape
    return sol.reshape((COMPS, *shape)), res.reshape((COMPS, *shape)), adj.reshape(shape)


def solution(mesh):
    placed = (
        P("diamond", "tile", None, None),
        P("diamond", "tile", None, None),
        P("diamond", "tile", None, None),
        P(None, "diamond", "tile", None, None),
        P(None, "diamond", "tile", None, None),
        P(),
        P(),
    )
    return jax.shard_map(
        body,
        mesh=mesh,
        in_specs=placed,
        out_specs=(
            P(None, "diamond", "tile", None, None),
            P(None, "diamond", "tile", None, None),
            P("diamond", "tile", None, None),
        ),
        check_vma=False,
    )
```

```python
import functools

import jax
import jax.numpy as jnp
from jax import lax
from jax.experimental import pallas as pl
from jax.experimental.pallas import tpu as pltpu
from jax.sharding import PartitionSpec as P

ITERS = 3
TIME_STEP = 0.1
DIFFUSION = 1.0
MASS_TERM = 0.5
BUOYANCY = 1.0

NY = 256
NR = 128
HALF = NY // 2
SPARE = 8
HELD = HALF + SPARE
COMPS = 3
MOMENTS = 2 * ITERS
MESH = pl.DeviceIdType.MESH
NX_CHIPS = 4
NY_CHIPS = 4
NZ_CHIPS = 32
Z_ROUNDS = 4
PLANE = NX_CHIPS * NY_CHIPS * 2


def device_at(x, y, z, core):
    return (lax.rem(x, 2), ((y * NZ_CHIPS + z) * 2 + x // 2) * 2 + core)


def shift(value, step, axis):
    return pltpu.roll(value, (-step) % value.shape[axis], axis)


def total_of(value):
    return jnp.sum(jnp.sum(value[0] + value[1], axis=0, keepdims=True), axis=1, keepdims=True)


def lane_row(entries):
    lane = lax.broadcasted_iota(jnp.int32, (1, NR), 1)
    row = jnp.zeros((1, NR), jnp.float32)
    for k, entry in enumerate(entries):
        row = row + jnp.where(lane == k, entry, 0.0)
    return row


def gradient_coefficients(mu):
    def inner(left, right):
        result = None
        for i, a in enumerate(left):
            for j, b in enumerate(right):
                term = a * b * mu[i + j]
                result = term if result is None else result + term
        return result

    one, zero = jnp.ones_like(mu[0]), jnp.zeros_like(mu[0])
    place, rest, direction = [zero] * ITERS, [one] + [zero] * ITERS, [one]
    now = mu[0]
    for step in range(ITERS):
        image = [direction[0]]
        for i in range(1, len(direction)):
            image.append(direction[i] - direction[i - 1])
        image.append(-direction[-1])
        size = now / inner(direction, image)
        for i, entry in enumerate(direction):
            place[i] = place[i] + size * entry
        for i, entry in enumerate(image):
            rest[i] = rest[i] - size * entry
        if step + 1 < ITERS:
            part = rest[: step + 2]
            later = inner(part, part)
            ratio = later / now
            direction = [part[i] + (ratio * direction[i] if i < len(direction) else 0.0) for i in range(len(part))]
            now = later
    return place, rest


def kernel(
    last,
    temp_in, misfit_in, visc_in, vel_in, forc_in, edge_in, pole_in,
    sol_out, res_out, adj_out,
    temp, misfit, vel, forc, tables, beside, moved, near, partner, vs, weights, diag, measure, adj, right, home, sol, onehot,
    zbuf, plane, mine,
    load_sem, store_sem, temp_send, temp_recv, move_send, move_recv, move_own, in_send, in_recv, out_send, out_recv,
    back_send, back_recv, small_send, small_recv, know,
):
    group = lax.axis_index("diamond")
    tile = lax.axis_index("tile")
    core = lax.rem(tile, 2)
    half = lax.rem(tile // 2, 2)
    quad = tile // 4
    x = half * 2 + group
    z = lax.rem(quad, NZ_CHIPS)
    y = quad // NZ_CHIPS
    first, final = tile == 0, tile == last
    opens = jnp.logical_and(quad == 0, core == 0)
    closes = jnp.logical_and(quad == last // 4, core == 1)
    at_end = jnp.logical_or(opens, closes)
    within = jnp.logical_not(at_end)
    outer_home = core == half

    def quad_dev(which_half, which_core):
        return (group, quad * 4 + which_half * 2 + which_core)

    def partner_dev(which_half):
        return (1 - group, quad * 4 + which_half * 2 + core)

    def x_dev(i):
        return device_at(x ^ i, y, z, core)

    def y_dev(i):
        return device_at(x, y ^ i, z, core)

    def z_dev(i):
        return device_at(x, y, lax.rem(z + i + NZ_CHIPS, NZ_CHIPS), core)

    inner_dev = quad_dev(half, 1 - core)
    outer_dev = (group, jnp.where(at_end, tile, jnp.where(core == 0, tile - 3, tile + 3)))
    before_dev = (jnp.where(first, 1 - group, group), jnp.where(first, 0, tile - 1))
    after_dev = (jnp.where(final, 1 - group, group), jnp.where(final, last, tile + 1))
    side_dev = (before_dev, after_dev)
    side_slot = (jnp.where(first, 0, 1), jnp.where(final, 1, 0))
    here = pl.ds(pl.multiple_of(half * HALF, HALF), HALF)
    held = pl.ds(pl.multiple_of(half * (HALF - SPARE), SPARE), HELD)
    core_lines = pl.ds(pl.multiple_of(half * SPARE, SPARE), HALF)

    loads = [
        pltpu.make_async_copy(source, target, load_sem.at[i])
        for i, (source, target) in enumerate(
            ((temp_in, temp), (misfit_in, misfit), (vel_in, vel), (forc_in, forc), (edge_in, tables.at[1]), (pole_in, tables.at[0]))
        )
    ]
    for load in loads:
        load.start()

    barrier = pltpu.get_barrier_semaphore()

    def greet(dev):
        pl.semaphore_signal(barrier, inc=1, device_id=dev, device_id_type=MESH)

    greeted = [inner_dev, quad_dev(1 - half, core), quad_dev(1 - half, 1 - core), x_dev(1), x_dev(3), y_dev(1), y_dev(3), z_dev(-1), z_dev(1)]
    for dev in greeted:
        greet(dev)
    home_beside = jnp.logical_and(outer_home, within)

    @pl.when(within)
    def _():
        greet(outer_dev)

    @pl.when(home_beside)
    def _():
        greet((group, jnp.where(core == 0, tile - 1, tile + 1)))

    @pl.when(at_end)
    def _():
        greet(partner_dev(0))
        greet(partner_dev(1))

    pl.semaphore_wait(barrier, len(greeted) + jnp.where(at_end, 2, jnp.where(home_beside, 2, 1)))

    def remote(source, target, send_sem, recv_sem, dev):
        return pltpu.make_async_remote_copy(
            src_ref=source, dst_ref=target, send_sem=send_sem, recv_sem=recv_sem, device_id=dev, device_id_type=MESH
        )

    def arrived(target, recv_sem):
        remote(target, target, temp_send.at[0], recv_sem, inner_dev).wait_recv()

    def temp_copy(side):
        return remote(temp_in, beside.at[side_slot[side]], temp_send.at[side], temp_recv.at[side_slot[side]], side_dev[side])

    sources = [visc_in, forc_in.at[0], forc_in.at[1], right]
    slot = jnp.where(outer_home, 0, 1)

    def move_copy(f, h):
        return remote(sources[f].at[pl.ds(h * (HALF - SPARE), HELD)], moved.at[f, slot], move_send.at[f, h], move_recv.at[f, slot], quad_dev(h, half))

    def own_copy(f):
        return pltpu.make_async_copy(sources[f].at[held], moved.at[f, 0], move_own.at[f])

    def move(f):
        for h in range(2):

            @pl.when(jnp.logical_not(jnp.logical_and(outer_home, half == h)))
            def _():
                move_copy(f, h).start()

        @pl.when(outer_home)
        def _():
            own_copy(f).start()

    def move_sent(f):
        for h in range(2):

            @pl.when(jnp.logical_not(jnp.logical_and(outer_home, half == h)))
            def _():
                move_copy(f, h).wait_send()

    def move_done(f):
        @pl.when(outer_home)
        def _():
            own_copy(f).wait()

        @pl.when(jnp.logical_not(outer_home))
        def _():
            arrived(moved.at[f, 0], move_recv.at[f, 0])

        arrived(moved.at[f, 1], move_recv.at[f, 1])

    def in_copy(s, c, rows):
        return remote(rows.at[1], near.at[s, c, 1], in_send.at[s, c], in_recv.at[s, c], inner_dev)

    def out_copy(s, c, rows):
        return remote(rows.at[0], near.at[s, c, 0], out_send.at[s, c, 0], out_recv.at[s, c, 0], outer_dev)

    def end_copy(s, c, rows, h):
        return remote(rows.at[0, core_lines], partner.at[s, c, here], out_send.at[s, c, h], out_recv.at[s, c, half], partner_dev(h))

    def give(s, c, rows):
        @pl.when(within)
        def _():
            out_copy(s, c, rows).start()

        @pl.when(at_end)
        def _():
            for h in range(2):
                end_copy(s, c, rows, h).start()

        in_copy(s, c, rows).start()

    def given(s, c, rows):
        @pl.when(within)
        def _():
            out_copy(s, c, rows).wait_send()

        @pl.when(at_end)
        def _():
            for h in range(2):
                end_copy(s, c, rows, h).wait_send()

        in_copy(s, c, rows).wait_send()

    def take(s, c):
        arrived(near.at[s, c, 1], in_recv.at[s, c])

        @pl.when(within)
        def _():
            arrived(near.at[s, c, 0], out_recv.at[s, c, 0])

        @pl.when(at_end)
        def _():
            for h in range(2):
                arrived(partner.at[s, c, pl.ds(h * HALF, HALF)], out_recv.at[s, c, h])
            near[s, c, 0] = jnp.dot(
                onehot[held, :], partner[s, c], precision=lax.Precision.HIGHEST, preferred_element_type=jnp.float32
            )

    def back_copy(a, rows, p):
        return remote(
            rows.at[p, core_lines], home.at[a, here], back_send.at[a, p], back_recv.at[a, half], quad_dev(core, (core, 1 - core)[p])
        )

    def give_back(a, rows):
        @pl.when(outer_home)
        def _():
            home[a, here, :] = rows[0, core_lines, :]

        @pl.when(jnp.logical_not(outer_home))
        def _():
            back_copy(a, rows, 0).start()

        back_copy(a, rows, 1).start()

    def back_sent(a, rows):
        @pl.when(jnp.logical_not(outer_home))
        def _():
            back_copy(a, rows, 0).wait_send()

        back_copy(a, rows, 1).wait_send()

    def back_done(a):
        for h in range(2):

            @pl.when(jnp.logical_not(jnp.logical_and(outer_home, half == h)))
            def _():
                arrived(home.at[a, pl.ds(h * HALF, HALF)], back_recv.at[a, h])

    for side in range(2):
        temp_copy(side).start()
    for f in range(3):
        move(f)

    def tell(round_, devs):
        for dev in devs:
            pl.semaphore_signal(know.at[round_], inc=1, device_id=dev, device_id_type=MESH)

    def hear(round_, count):
        pl.semaphore_wait(know.at[round_], count)

    tell(0, (z_dev(-1), z_dev(1)))
    tell(Z_ROUNDS, (x_dev(1), x_dev(3)))
    tell(Z_ROUNDS + 1, (y_dev(1), y_dev(3)))

    loads[4].wait()
    loads[5].wait()

    for at, end in enumerate((opens, closes)):

        @pl.when(end)
        def _():
            inverse = jnp.where(group == 0, tables[at, 1:2, :], tables[at, 0:1, :])
            place = lax.broadcasted_iota(jnp.int32, (NY, NY), 0)
            onehot[...] = jnp.where(place == inverse, 1.0, 0.0).astype(jnp.float32)

    for load in loads[:4]:
        load.wait()
    y_place = lax.broadcasted_iota(jnp.int32, (NY, NR), 0)
    r_place = lax.broadcasted_iota(jnp.int32, (NY, NR), 1)
    inside = (y_place < NY - 1, y_place > 0, r_place < NR - 1, r_place > 0)
    own = temp[...]
    other = [jnp.where(inside[k], shift(own, step, axis), 0.0) for k, (step, axis) in enumerate(((1, 0), (-1, 0), (1, 1), (-1, 1)))]
    adj[...] = own + misfit[...] + TIME_STEP * (
        DIFFUSION * (other[0] + other[1] + other[2] + other[3] - 6.0 * own)
        + 0.5 * (vel[1] * (other[0] - other[1]) + vel[2] * (other[2] - other[3]))
    )
    hear(0, 2)
    tell(1, (z_dev(-2), z_dev(2)))
    for side in range(2):
        arrived(beside.at[side], temp_recv.at[side])

        @pl.when((first, final)[side])
        def _():
            beside[side] = jnp.dot(onehot[...], beside[side], precision=lax.Precision.HIGHEST, preferred_element_type=jnp.float32)

    after, before = beside[1], beside[0]
    adj[...] = adj[...] + TIME_STEP * (DIFFUSION * (after + before) + 0.5 * (vel[0] * (after - before)))
    right[...] = forc[COMPS - 1] + BUOYANCY * adj[...]
    move(3)
    adj_store = pltpu.make_async_copy(adj, adj_out, store_sem.at[2 * COMPS])
    adj_store.start()
    hear(1, 2)
    tell(2, (z_dev(-4), z_dev(4)))
    hear(Z_ROUNDS, 2)
    hear(Z_ROUNDS + 1, 2)
    tell(Z_ROUNDS + 2, (y_dev(2), y_dev(1), y_dev(3)))

    moves = ((1, 1), (-1, 1), (1, 2), (-1, 2))
    shape = (2, HELD, NR)
    y_place = lax.broadcasted_iota(jnp.int32, shape, 1)
    r_place = lax.broadcasted_iota(jnp.int32, shape, 2)
    inside = (y_place < HELD - 1, y_place > 0, r_place < NR - 1, r_place > 0)
    spare_at = (1 - half) * HALF
    counts = jnp.logical_or(y_place < spare_at, y_place >= spare_at + SPARE)
    move_done(0)
    visc = moved.at[0]
    give(ITERS, 0, visc)
    own = visc[...]
    local = jnp.full(shape, MASS_TERM, jnp.float32)
    for k, (step, axis) in enumerate(moves):
        weight = jnp.where(inside[k], 0.5 * (own + shift(own, step, axis)), 0.0)
        weights[k] = weight
        local = local + weight
    between = 0.5 * (own[0] + own[1])
    for p in range(2):
        weights[4, p] = between
    diag[...] = local + weights[4]
    take(ITERS, 0)
    outside = 0.5 * (visc[...] + near[ITERS, 0])
    diagonal = diag[...] + outside
    diag[...] = diagonal
    measure[...] = jnp.where(counts, diagonal, 0.0)
    inverse_diagonal = 1.0 / diagonal
    weights[5] = outside * inverse_diagonal
    for k in range(5):
        weights[k] = weights[k] * inverse_diagonal
    for c in range(COMPS):
        if c + 1 == COMPS:
            hear(2, 2)
            tell(3, (z_dev(-8), z_dev(8)))
        move_done(1 + c)
        vs[0, c] = moved[1 + c] / diag[...]
        give(0, c, vs.at[0, c])

    end_quad = jnp.logical_or(quad == 0, quad == last // 4)


    @pl.when(jnp.logical_not(end_quad))
    def _():
        give_back(0, diag)

    mu = []
    for step in range(ITERS):
        for c in range(COMPS):
            value = vs[step, c]
            result = weights[4, 0] * value[1], weights[4, 1] * value[0]
            vs[step + 1, c, 0] = result[0]
            vs[step + 1, c, 1] = result[1]
            part = vs[step + 1, c]
            for k, (move_by, axis) in enumerate(moves):
                part = part + weights[k] * shift(value, move_by, axis)
            vs[step + 1, c] = part
        mu.append(total_of(measure[...] * sum(vs[step, c] * vs[step, c] for c in range(COMPS))))
        odd = None
        for c in range(COMPS):
            take(step, c)
            vs[step + 1, c] = vs[step + 1, c] + weights[5] * near[step, c]
            if step + 1 < ITERS:
                give(step + 1, c, vs.at[step + 1, c])
            term = vs[step, c] * vs[step + 1, c]
            odd = term if odd is None else odd + term
        mu.append(total_of(measure[...] * odd))
        if step + 1 < ITERS:
            if step == 0:
                hear(Z_ROUNDS + 2, 3)
                tell(Z_ROUNDS + 3, (inner_dev,))

            if step == 0:

                @pl.when(jnp.logical_not(end_quad))
                def _():
                    for c in range(COMPS):
                        give_back(1 + c, vs.at[1, c])

            if step:

                @pl.when(jnp.logical_not(end_quad))
                def _():
                    for c in range(COMPS):
                        give_back(1 + COMPS + c, vs.at[2, c])

                hear(Z_ROUNDS - 1, 2)
                tell(Z_ROUNDS + 4, (inner_dev,))

    def small_copy(i, buffer, slot, dev):
        return remote(mine, buffer.at[slot], small_send.at[i], small_recv.at[i], dev)

    def gather(i, buffer, count):
        part = buffer.at[pl.ds(0, count)]
        whole = remote(part, part, small_send.at[i], small_recv.at[i], inner_dev)
        whole.wait_send()
        whole.wait_recv()
        mine[...] = jnp.sum(buffer[...], axis=0)

    mine[...] = lane_row(mu)
    hear(Z_ROUNDS + 4, 1)

    def z_send(i, carry):
        k = (i + 1) // 2
        offset = NZ_CHIPS // 2 + k * (1 - 2 * lax.rem(i, 2))
        dev = device_at(x, y, lax.rem(z + offset, NZ_CHIPS), 1 - core)
        small_copy(0, zbuf, z, dev).start()
        return carry

    lax.fori_loop(0, NZ_CHIPS, z_send, 0)

    @pl.when(end_quad)
    def _():
        give_back(0, diag)
        for c in range(COMPS):
            give_back(1 + c, vs.at[1, c])
            give_back(1 + COMPS + c, vs.at[2, c])

    for c in range(COMPS):
        give_back(1 + 2 * COMPS + c, vs.at[3, c])
    hear(Z_ROUNDS + 3, 1)
    gather(0, zbuf, NZ_CHIPS)
    plane_slot = (y * NX_CHIPS + x) * 2 + core
    plane[plane_slot] = mine[...]

    def plane_send(i, carry):
        k = PLANE - 1 - i
        dev = device_at(x ^ lax.rem(k // 2, NX_CHIPS), y ^ (k // (2 * NX_CHIPS)), z, core ^ lax.rem(k, 2))
        small_copy(1, plane, plane_slot, dev).start()
        return carry

    lax.fori_loop(0, PLANE - 1, plane_send, 0)
    for a in range(1 + ITERS * COMPS):
        back_done(a)
    gather(1, plane, PLANE - 1)
    sums = mine[...]
    place, rest = gradient_coefficients([sums[:, k : k + 1] for k in range(MOMENTS)])
    stores = [adj_store]
    for c in range(COMPS):
        full = forc[c] if c + 1 < COMPS else right[...]
        krylov = [full / home[0]] + [home[1 + step * COMPS + c] for step in range(ITERS)]
        sol[0, c] = sum(place[k] * krylov[k] for k in range(ITERS))
        sol[1, c] = rest[0] * full + home[0] * sum(rest[k] * krylov[k] for k in range(1, ITERS + 1))
        for at, out in enumerate((sol_out, res_out)):
            store = pltpu.make_async_copy(sol.at[at, c], out.at[c], store_sem.at[at * COMPS + c])
            store.start()
            stores.append(store)

    for side in range(2):
        temp_copy(side).wait_send()
    for f in range(1 + COMPS):
        move_sent(f)
    given(ITERS, 0, visc)
    back_sent(0, diag)
    for s in range(ITERS):
        for c in range(COMPS):
            given(s, c, vs.at[s, c])
            back_sent(1 + s * COMPS + c, vs.at[s + 1, c])
    for store in stores:
        store.wait()


def body(adjoint_temp, misfit, viscosity, velocity, forcing, edge_table, pole_table):
    row = (NY, NR)
    rows = (COMPS, NY, NR)
    pair = (2, HELD, NR)
    f32 = jnp.float32
    dma = pltpu.SemaphoreType.DMA
    any_space = pl.BlockSpec(memory_space=pl.ANY)
    sol, res, adj = pl.pallas_call(
        functools.partial(kernel, lax.axis_size("tile") - 1),
        out_shape=(
            pltpu.VMEM(rows, f32),
            pltpu.VMEM(rows, f32),
            pltpu.VMEM(row, f32),
        ),
        in_specs=[any_space] * 7,
        out_specs=(any_space,) * 3,
        scratch_shapes=[
            pltpu.VMEM(row, f32),
            pltpu.VMEM(row, f32),
            pltpu.VMEM(rows, f32),
            pltpu.VMEM(rows, f32),
            pltpu.VMEM((2, 2, NY), jnp.int32),
            pltpu.VMEM((2, *row), f32),
            pltpu.VMEM((1 + COMPS, *pair), f32),
            pltpu.VMEM((ITERS + 1, COMPS, *pair), f32),
            pltpu.VMEM((ITERS + 1, COMPS, *row), f32),
            pltpu.VMEM((ITERS + 1, COMPS, *pair), f32),
            pltpu.VMEM((6, *pair), f32),
            pltpu.VMEM(pair, f32),
            pltpu.VMEM(pair, f32),
            pltpu.VMEM(row, f32),
            pltpu.VMEM(row, f32),
            pltpu.VMEM((1 + ITERS * COMPS, *row), f32),
            pltpu.VMEM((2, *rows), f32),
            pltpu.VMEM((NY, NY), f32),
            pltpu.VMEM((NZ_CHIPS, 1, NR), f32),
            pltpu.VMEM((PLANE, 1, NR), f32),
            pltpu.VMEM((1, NR), f32),
            dma((6,)),
            dma((1 + 2 * COMPS,)),
            dma((2,)),
            dma((2,)),
            dma((1 + COMPS, 2)),
            dma((1 + COMPS, 2)),
            dma((1 + COMPS,)),
            dma((ITERS + 1, COMPS)),
            dma((ITERS + 1, COMPS)),
            dma((ITERS + 1, COMPS, 2)),
            dma((ITERS + 1, COMPS, 2)),
            dma((1 + ITERS * COMPS, 2)),
            dma((1 + ITERS * COMPS, 2)),
            dma((2,)),
            dma((2,)),
            pltpu.SemaphoreType.REGULAR((Z_ROUNDS + 5,)),
        ],
        compiler_params=pltpu.CompilerParams(collective_id=0, has_side_effects=True, vmem_limit_bytes=60 << 20),
    )(
        adjoint_temp.reshape(row),
        misfit.reshape(row),
        viscosity.reshape(row),
        velocity.reshape(rows),
        forcing.reshape(rows),
        edge_table,
        pole_table,
    )
    shape = adjoint_temp.shape
    return sol.reshape((COMPS, *shape)), res.reshape((COMPS, *shape)), adj.reshape(shape)


def solution(mesh):
    placed = (
        P("diamond", "tile", None, None),
        P("diamond", "tile", None, None),
        P("diamond", "tile", None, None),
        P(None, "diamond", "tile", None, None),
        P(None, "diamond", "tile", None, None),
        P(),
        P(),
    )
    return jax.shard_map(
        body,
        mesh=mesh,
        in_specs=placed,
        out_specs=(
            P(None, "diamond", "tile", None, None),
            P(None, "diamond", "tile", None, None),
            P("diamond", "tile", None, None),
        ),
        check_vma=False,
    )
```

```python
import functools

import jax
import jax.numpy as jnp
from jax import lax
from jax.experimental import pallas as pl
from jax.experimental.pallas import tpu as pltpu
from jax.sharding import PartitionSpec as P

ITERS = 3
TIME_STEP = 0.1
DIFFUSION = 1.0
MASS_TERM = 0.5
BUOYANCY = 1.0

NY = 256
NR = 128
HALF = NY // 2
SPARE = 8
HELD = HALF + SPARE
COMPS = 3
MOMENTS = 2 * ITERS
MESH = pl.DeviceIdType.MESH
NX_CHIPS = 4
NY_CHIPS = 4
NZ_CHIPS = 32
Z_ROUNDS = 4
PLANE = NX_CHIPS * NY_CHIPS * 2


def device_at(x, y, z, core):
    return (lax.rem(x, 2), ((y * NZ_CHIPS + z) * 2 + x // 2) * 2 + core)


def shift(value, step, axis):
    return pltpu.roll(value, (-step) % value.shape[axis], axis)


def total_of(value):
    return jnp.sum(jnp.sum(value[0] + value[1], axis=0, keepdims=True), axis=1, keepdims=True)


def lane_row(entries):
    lane = lax.broadcasted_iota(jnp.int32, (1, NR), 1)
    row = jnp.zeros((1, NR), jnp.float32)
    for k, entry in enumerate(entries):
        row = row + jnp.where(lane == k, entry, 0.0)
    return row


def gradient_coefficients(mu):
    def inner(left, right):
        result = None
        for i, a in enumerate(left):
            for j, b in enumerate(right):
                term = a * b * mu[i + j]
                result = term if result is None else result + term
        return result

    one, zero = jnp.ones_like(mu[0]), jnp.zeros_like(mu[0])
    place, rest, direction = [zero] * ITERS, [one] + [zero] * ITERS, [one]
    now = mu[0]
    for step in range(ITERS):
        image = [direction[0]]
        for i in range(1, len(direction)):
            image.append(direction[i] - direction[i - 1])
        image.append(-direction[-1])
        size = now / inner(direction, image)
        for i, entry in enumerate(direction):
            place[i] = place[i] + size * entry
        for i, entry in enumerate(image):
            rest[i] = rest[i] - size * entry
        if step + 1 < ITERS:
            part = rest[: step + 2]
            later = inner(part, part)
            ratio = later / now
            direction = [part[i] + (ratio * direction[i] if i < len(direction) else 0.0) for i in range(len(part))]
            now = later
    return place, rest


def kernel(
    last,
    temp_in, misfit_in, visc_in, vel_in, forc_in, edge_in, pole_in,
    sol_out, res_out, adj_out,
    temp, misfit, vel, forc, tables, beside, moved, near, partner, vs, weights, diag, measure, adj, right, home, sol, onehot,
    zbuf, plane, mine,
    load_sem, store_sem, temp_send, temp_recv, move_send, move_recv, move_own, in_send, in_recv, out_send, out_recv,
    back_send, back_recv, small_send, small_recv, know,
):
    group = lax.axis_index("diamond")
    tile = lax.axis_index("tile")
    core = lax.rem(tile, 2)
    half = lax.rem(tile // 2, 2)
    quad = tile // 4
    x = half * 2 + group
    z = lax.rem(quad, NZ_CHIPS)
    y = quad // NZ_CHIPS
    first, final = tile == 0, tile == last
    opens = jnp.logical_and(quad == 0, core == 0)
    closes = jnp.logical_and(quad == last // 4, core == 1)
    at_end = jnp.logical_or(opens, closes)
    within = jnp.logical_not(at_end)
    outer_home = core == half

    def quad_dev(which_half, which_core):
        return (group, quad * 4 + which_half * 2 + which_core)

    def partner_dev(which_half):
        return (1 - group, quad * 4 + which_half * 2 + core)

    def x_dev(i):
        return device_at(x ^ i, y, z, core)

    def y_dev(i):
        return device_at(x, y ^ i, z, core)

    def z_dev(i):
        return device_at(x, y, lax.rem(z + i + NZ_CHIPS, NZ_CHIPS), core)

    inner_dev = quad_dev(half, 1 - core)
    outer_dev = (group, jnp.where(at_end, tile, jnp.where(core == 0, tile - 3, tile + 3)))
    before_dev = (jnp.where(first, 1 - group, group), jnp.where(first, 0, tile - 1))
    after_dev = (jnp.where(final, 1 - group, group), jnp.where(final, last, tile + 1))
    side_dev = (before_dev, after_dev)
    side_slot = (jnp.where(first, 0, 1), jnp.where(final, 1, 0))
    here = pl.ds(pl.multiple_of(half * HALF, HALF), HALF)
    held = pl.ds(pl.multiple_of(half * (HALF - SPARE), SPARE), HELD)
    core_lines = pl.ds(pl.multiple_of(half * SPARE, SPARE), HALF)

    loads = [
        pltpu.make_async_copy(source, target, load_sem.at[i])
        for i, (source, target) in enumerate(
            ((temp_in, temp), (misfit_in, misfit), (vel_in, vel), (forc_in, forc), (edge_in, tables.at[1]), (pole_in, tables.at[0]))
        )
    ]
    for load in loads:
        load.start()

    barrier = pltpu.get_barrier_semaphore()

    def greet(dev):
        pl.semaphore_signal(barrier, inc=1, device_id=dev, device_id_type=MESH)

    greeted = [inner_dev, quad_dev(1 - half, core), quad_dev(1 - half, 1 - core), x_dev(1), x_dev(3), y_dev(1), y_dev(3), z_dev(-1), z_dev(1)]
    for dev in greeted:
        greet(dev)
    home_beside = jnp.logical_and(outer_home, within)

    @pl.when(within)
    def _():
        greet(outer_dev)

    @pl.when(home_beside)
    def _():
        greet((group, jnp.where(core == 0, tile - 1, tile + 1)))

    @pl.when(at_end)
    def _():
        greet(partner_dev(0))
        greet(partner_dev(1))

    pl.semaphore_wait(barrier, len(greeted) + jnp.where(at_end, 2, jnp.where(home_beside, 2, 1)))

    def remote(source, target, send_sem, recv_sem, dev):
        return pltpu.make_async_remote_copy(
            src_ref=source, dst_ref=target, send_sem=send_sem, recv_sem=recv_sem, device_id=dev, device_id_type=MESH
        )

    def arrived(target, recv_sem):
        remote(target, target, temp_send.at[0], recv_sem, inner_dev).wait_recv()

    def temp_copy(side):
        return remote(temp_in, beside.at[side_slot[side]], temp_send.at[side], temp_recv.at[side_slot[side]], side_dev[side])

    sources = [visc_in, forc_in.at[0], forc_in.at[1], right]
    slot = jnp.where(outer_home, 0, 1)

    def move_copy(f, h):
        return remote(sources[f].at[pl.ds(h * (HALF - SPARE), HELD)], moved.at[f, slot], move_send.at[f, h], move_recv.at[f, slot], quad_dev(h, half))

    def own_copy(f):
        return pltpu.make_async_copy(sources[f].at[held], moved.at[f, 0], move_own.at[f])

    def move(f):
        for h in range(2):

            @pl.when(jnp.logical_not(jnp.logical_and(outer_home, half == h)))
            def _():
                move_copy(f, h).start()

        @pl.when(outer_home)
        def _():
            own_copy(f).start()

    def move_sent(f):
        for h in range(2):

            @pl.when(jnp.logical_not(jnp.logical_and(outer_home, half == h)))
            def _():
                move_copy(f, h).wait_send()

    def move_done(f):
        @pl.when(outer_home)
        def _():
            own_copy(f).wait()

        @pl.when(jnp.logical_not(outer_home))
        def _():
            arrived(moved.at[f, 0], move_recv.at[f, 0])

        arrived(moved.at[f, 1], move_recv.at[f, 1])

    def in_copy(s, c, rows):
        return remote(rows.at[1], near.at[s, c, 1], in_send.at[s, c], in_recv.at[s, c], inner_dev)

    def out_copy(s, c, rows):
        return remote(rows.at[0], near.at[s, c, 0], out_send.at[s, c, 0], out_recv.at[s, c, 0], outer_dev)

    def end_copy(s, c, rows, h):
        return remote(rows.at[0, core_lines], partner.at[s, c, here], out_send.at[s, c, h], out_recv.at[s, c, half], partner_dev(h))

    def give(s, c, rows):
        @pl.when(within)
        def _():
            out_copy(s, c, rows).start()

        @pl.when(at_end)
        def _():
            for h in range(2):
                end_copy(s, c, rows, h).start()

        in_copy(s, c, rows).start()

    def given(s, c, rows):
        @pl.when(within)
        def _():
            out_copy(s, c, rows).wait_send()

        @pl.when(at_end)
        def _():
            for h in range(2):
                end_copy(s, c, rows, h).wait_send()

        in_copy(s, c, rows).wait_send()

    def take(s, c):
        arrived(near.at[s, c, 1], in_recv.at[s, c])

        @pl.when(within)
        def _():
            arrived(near.at[s, c, 0], out_recv.at[s, c, 0])

        @pl.when(at_end)
        def _():
            for h in range(2):
                arrived(partner.at[s, c, pl.ds(h * HALF, HALF)], out_recv.at[s, c, h])
            near[s, c, 0] = jnp.dot(
                onehot[held, :], partner[s, c], precision=lax.Precision.HIGHEST, preferred_element_type=jnp.float32
            )

    def back_copy(a, rows, p):
        return remote(
            rows.at[p, core_lines], home.at[a, here], back_send.at[a, p], back_recv.at[a, half], quad_dev(core, (core, 1 - core)[p])
        )

    def give_back(a, rows):
        @pl.when(outer_home)
        def _():
            home[a, here, :] = rows[0, core_lines, :]

        @pl.when(jnp.logical_not(outer_home))
        def _():
            back_copy(a, rows, 0).start()

        back_copy(a, rows, 1).start()

    def back_sent(a, rows):
        @pl.when(jnp.logical_not(outer_home))
        def _():
            back_copy(a, rows, 0).wait_send()

        back_copy(a, rows, 1).wait_send()

    def back_done(a):
        for h in range(2):

            @pl.when(jnp.logical_not(jnp.logical_and(outer_home, half == h)))
            def _():
                arrived(home.at[a, pl.ds(h * HALF, HALF)], back_recv.at[a, h])

    for side in range(2):
        temp_copy(side).start()
    for f in range(3):
        move(f)

    def tell(round_, devs):
        for dev in devs:
            pl.semaphore_signal(know.at[round_], inc=1, device_id=dev, device_id_type=MESH)

    def hear(round_, count):
        pl.semaphore_wait(know.at[round_], count)

    tell(0, (z_dev(-1), z_dev(1)))
    tell(Z_ROUNDS, (x_dev(1), x_dev(3)))
    tell(Z_ROUNDS + 1, (y_dev(1), y_dev(3)))

    loads[4].wait()
    loads[5].wait()

    for at, end in enumerate((opens, closes)):

        @pl.when(end)
        def _():
            inverse = jnp.where(group == 0, tables[at, 1:2, :], tables[at, 0:1, :])
            place = lax.broadcasted_iota(jnp.int32, (NY, NY), 0)
            onehot[...] = jnp.where(place == inverse, 1.0, 0.0).astype(jnp.float32)

    for load in loads[:4]:
        load.wait()
    y_place = lax.broadcasted_iota(jnp.int32, (NY, NR), 0)
    r_place = lax.broadcasted_iota(jnp.int32, (NY, NR), 1)
    inside = (y_place < NY - 1, y_place > 0, r_place < NR - 1, r_place > 0)
    own = temp[...]
    other = [jnp.where(inside[k], shift(own, step, axis), 0.0) for k, (step, axis) in enumerate(((1, 0), (-1, 0), (1, 1), (-1, 1)))]
    adj[...] = own + misfit[...] + TIME_STEP * (
        DIFFUSION * (other[0] + other[1] + other[2] + other[3] - 6.0 * own)
        + 0.5 * (vel[1] * (other[0] - other[1]) + vel[2] * (other[2] - other[3]))
    )
    hear(0, 2)
    tell(1, (z_dev(-2), z_dev(2)))
    for side in range(2):
        arrived(beside.at[side], temp_recv.at[side])

        @pl.when((first, final)[side])
        def _():
            beside[side] = jnp.dot(onehot[...], beside[side], precision=lax.Precision.HIGHEST, preferred_element_type=jnp.float32)

    after, before = beside[1], beside[0]
    adj[...] = adj[...] + TIME_STEP * (DIFFUSION * (after + before) + 0.5 * (vel[0] * (after - before)))
    right[...] = forc[COMPS - 1] + BUOYANCY * adj[...]
    move(3)
    adj_store = pltpu.make_async_copy(adj, adj_out, store_sem.at[2 * COMPS])
    adj_store.start()
    hear(1, 2)
    tell(2, (z_dev(-4), z_dev(4)))
    hear(Z_ROUNDS, 2)
    hear(Z_ROUNDS + 1, 2)
    tell(Z_ROUNDS + 2, (y_dev(2), y_dev(1), y_dev(3)))

    moves = ((1, 1), (-1, 1), (1, 2), (-1, 2))
    shape = (2, HELD, NR)
    y_place = lax.broadcasted_iota(jnp.int32, shape, 1)
    r_place = lax.broadcasted_iota(jnp.int32, shape, 2)
    inside = (y_place < HELD - 1, y_place > 0, r_place < NR - 1, r_place > 0)
    spare_at = (1 - half) * HALF
    counts = jnp.logical_or(y_place < spare_at, y_place >= spare_at + SPARE)
    move_done(0)
    visc = moved.at[0]
    give(ITERS, 0, visc)
    own = visc[...]
    local = jnp.full(shape, MASS_TERM, jnp.float32)
    for k, (step, axis) in enumerate(moves):
        weight = jnp.where(inside[k], 0.5 * (own + shift(own, step, axis)), 0.0)
        weights[k] = weight
        local = local + weight
    between = 0.5 * (own[0] + own[1])
    for p in range(2):
        weights[4, p] = between
    diag[...] = local + weights[4]
    take(ITERS, 0)
    outside = 0.5 * (visc[...] + near[ITERS, 0])
    diagonal = diag[...] + outside
    diag[...] = diagonal
    measure[...] = jnp.where(counts, diagonal, 0.0)
    inverse_diagonal = 1.0 / diagonal
    weights[5] = outside * inverse_diagonal
    for k in range(5):
        weights[k] = weights[k] * inverse_diagonal
    for c in range(COMPS):
        if c + 1 == COMPS:
            hear(2, 2)
            tell(3, (z_dev(-8), z_dev(8)))
        move_done(1 + c)
        vs[0, c] = moved[1 + c] / diag[...]
        give(0, c, vs.at[0, c])

    end_quad = jnp.logical_or(quad == 0, quad == last // 4)


    @pl.when(jnp.logical_not(end_quad))
    def _():
        give_back(0, diag)

    mu = []
    for step in range(ITERS):
        for c in range(COMPS):
            value = vs[step, c]
            result = weights[4, 0] * value[1], weights[4, 1] * value[0]
            vs[step + 1, c, 0] = result[0]
            vs[step + 1, c, 1] = result[1]
            part = vs[step + 1, c]
            for k, (move_by, axis) in enumerate(moves):
                part = part + weights[k] * shift(value, move_by, axis)
            vs[step + 1, c] = part
        mu.append(total_of(measure[...] * sum(vs[step, c] * vs[step, c] for c in range(COMPS))))
        odd = None
        for c in range(COMPS):
            take(step, c)
            vs[step + 1, c] = vs[step + 1, c] + weights[5] * near[step, c]
            if step + 1 < ITERS:
                give(step + 1, c, vs.at[step + 1, c])
            term = vs[step, c] * vs[step + 1, c]
            odd = term if odd is None else odd + term
        mu.append(total_of(measure[...] * odd))
        if step + 1 < ITERS:
            if step == 0:
                hear(Z_ROUNDS + 2, 3)
                tell(Z_ROUNDS + 3, (inner_dev,))

            if step == 0:

                @pl.when(jnp.logical_not(end_quad))
                def _():
                    for c in range(COMPS):
                        give_back(1 + c, vs.at[1, c])

            if step:

                @pl.when(jnp.logical_not(end_quad))
                def _():
                    for c in range(COMPS):
                        give_back(1 + COMPS + c, vs.at[2, c])

                hear(Z_ROUNDS - 1, 2)
                tell(Z_ROUNDS + 4, (inner_dev,))

    def small_copy(i, buffer, slot, dev):
        return remote(mine, buffer.at[slot], small_send.at[i], small_recv.at[i], dev)

    def gather(i, buffer, count):
        part = buffer.at[pl.ds(0, count)]
        whole = remote(part, part, small_send.at[i], small_recv.at[i], inner_dev)
        whole.wait_send()
        whole.wait_recv()
        mine[...] = jnp.sum(buffer[...], axis=0)

    mine[...] = lane_row(mu)
    hear(Z_ROUNDS + 4, 1)

    def z_send(i, carry):
        k = (i + 1) // 2
        offset = NZ_CHIPS // 2 + k * (1 - 2 * lax.rem(i, 2))
        dev = device_at(x, y, lax.rem(z + offset, NZ_CHIPS), 1 - core)
        small_copy(0, zbuf, z, dev).start()
        return carry

    lax.fori_loop(0, NZ_CHIPS, z_send, 0)

    @pl.when(end_quad)
    def _():
        give_back(0, diag)
        for c in range(COMPS):
            give_back(1 + c, vs.at[1, c])
            give_back(1 + COMPS + c, vs.at[2, c])

    for c in range(COMPS):
        give_back(1 + 2 * COMPS + c, vs.at[3, c])
    hear(Z_ROUNDS + 3, 1)
    gather(0, zbuf, NZ_CHIPS)
    plane_slot = (y * NX_CHIPS + x) * 2 + core
    plane[plane_slot] = mine[...]

    def plane_send(i, carry):
        k = PLANE - 1 - i
        dev = device_at(x ^ lax.rem(k // 2, NX_CHIPS), y ^ (k // (2 * NX_CHIPS)), z, core ^ lax.rem(k, 2))
        small_copy(1, plane, plane_slot, dev).start()
        return carry

    lax.fori_loop(0, PLANE - 1, plane_send, 0)
    for a in range(1 + ITERS * COMPS):
        back_done(a)
    for c in range(COMPS):
        vel[c] = (forc[c] if c + 1 < COMPS else right[...]) / home[0]
    gather(1, plane, PLANE - 1)
    sums = mine[...]
    place, rest = gradient_coefficients([sums[:, k : k + 1] for k in range(MOMENTS)])
    stores = [adj_store]
    for c in range(COMPS):
        full = forc[c] if c + 1 < COMPS else right[...]
        krylov = [vel[c]] + [home[1 + step * COMPS + c] for step in range(ITERS)]
        sol[0, c] = sum(place[k] * krylov[k] for k in range(ITERS))
        sol[1, c] = rest[0] * full + home[0] * sum(rest[k] * krylov[k] for k in range(1, ITERS + 1))
        for at, out in enumerate((sol_out, res_out)):
            store = pltpu.make_async_copy(sol.at[at, c], out.at[c], store_sem.at[at * COMPS + c])
            store.start()
            stores.append(store)

    for side in range(2):
        temp_copy(side).wait_send()
    for f in range(1 + COMPS):
        move_sent(f)
    given(ITERS, 0, visc)
    back_sent(0, diag)
    for s in range(ITERS):
        for c in range(COMPS):
            given(s, c, vs.at[s, c])
            back_sent(1 + s * COMPS + c, vs.at[s + 1, c])
    for store in stores:
        store.wait()


def body(adjoint_temp, misfit, viscosity, velocity, forcing, edge_table, pole_table):
    row = (NY, NR)
    rows = (COMPS, NY, NR)
    pair = (2, HELD, NR)
    f32 = jnp.float32
    dma = pltpu.SemaphoreType.DMA
    any_space = pl.BlockSpec(memory_space=pl.ANY)
    sol, res, adj = pl.pallas_call(
        functools.partial(kernel, lax.axis_size("tile") - 1),
        out_shape=(
            pltpu.VMEM(rows, f32),
            pltpu.VMEM(rows, f32),
            pltpu.VMEM(row, f32),
        ),
        in_specs=[any_space] * 7,
        out_specs=(any_space,) * 3,
        scratch_shapes=[
            pltpu.VMEM(row, f32),
            pltpu.VMEM(row, f32),
            pltpu.VMEM(rows, f32),
            pltpu.VMEM(rows, f32),
            pltpu.VMEM((2, 2, NY), jnp.int32),
            pltpu.VMEM((2, *row), f32),
            pltpu.VMEM((1 + COMPS, *pair), f32),
            pltpu.VMEM((ITERS + 1, COMPS, *pair), f32),
            pltpu.VMEM((ITERS + 1, COMPS, *row), f32),
            pltpu.VMEM((ITERS + 1, COMPS, *pair), f32),
            pltpu.VMEM((6, *pair), f32),
            pltpu.VMEM(pair, f32),
            pltpu.VMEM(pair, f32),
            pltpu.VMEM(row, f32),
            pltpu.VMEM(row, f32),
            pltpu.VMEM((1 + ITERS * COMPS, *row), f32),
            pltpu.VMEM((2, *rows), f32),
            pltpu.VMEM((NY, NY), f32),
            pltpu.VMEM((NZ_CHIPS, 1, NR), f32),
            pltpu.VMEM((PLANE, 1, NR), f32),
            pltpu.VMEM((1, NR), f32),
            dma((6,)),
            dma((1 + 2 * COMPS,)),
            dma((2,)),
            dma((2,)),
            dma((1 + COMPS, 2)),
            dma((1 + COMPS, 2)),
            dma((1 + COMPS,)),
            dma((ITERS + 1, COMPS)),
            dma((ITERS + 1, COMPS)),
            dma((ITERS + 1, COMPS, 2)),
            dma((ITERS + 1, COMPS, 2)),
            dma((1 + ITERS * COMPS, 2)),
            dma((1 + ITERS * COMPS, 2)),
            dma((2,)),
            dma((2,)),
            pltpu.SemaphoreType.REGULAR((Z_ROUNDS + 5,)),
        ],
        compiler_params=pltpu.CompilerParams(collective_id=0, has_side_effects=True, vmem_limit_bytes=60 << 20),
    )(
        adjoint_temp.reshape(row),
        misfit.reshape(row),
        viscosity.reshape(row),
        velocity.reshape(rows),
        forcing.reshape(rows),
        edge_table,
        pole_table,
    )
    shape = adjoint_temp.shape
    return sol.reshape((COMPS, *shape)), res.reshape((COMPS, *shape)), adj.reshape(shape)


def solution(mesh):
    placed = (
        P("diamond", "tile", None, None),
        P("diamond", "tile", None, None),
        P("diamond", "tile", None, None),
        P(None, "diamond", "tile", None, None),
        P(None, "diamond", "tile", None, None),
        P(),
        P(),
    )
    return jax.shard_map(
        body,
        mesh=mesh,
        in_specs=placed,
        out_specs=(
            P(None, "diamond", "tile", None, None),
            P(None, "diamond", "tile", None, None),
            P("diamond", "tile", None, None),
        ),
        check_vma=False,
    )
```
